256 devices in a mesh: row: 16 (over x, z_hi), col: 8 (over z_lo, y), snode: 2 (over core).
Axes of the slice: x: 4, y: 4, z: 8 (z_hi: 4, z_lo: 2; z = z_hi * 2 + z_lo), core: 2. Of those that a mesh axis runs over, the one named last changes fastest.
Arguments:
- ancestor_inverse: bfloat16 [40960, 20480], P(('snode', 'row'), 'col'), parts along dimension 0, may hold values from -8 to 8
- fill_mask: int32 [160, 80], P('snode'), parts along dimension 0, may hold values from 0 to 1, as said below
- block_order: int32 [4, 80], P('snode'), parts along dimension 0, may hold values from 0 to 79, each once within a row
- l_rows: bfloat16 [4, 20480, 256], P('snode', ('row', 'col')), parts along dimension 0, may hold values from -6 to 6
- diag_inverse: bfloat16 [4, 256, 256], P('snode'), parts along dimension 0, may hold values from -0.0024414062 to 0.0024414062
Outputs:
- ainv_kr: bfloat16 [4, 256, 20480], P('snode', None, ('row', 'col')), parts along dimension 0
The draws below stay inside these ranges and needn't reach their ends.
There are 2 independent parts, one for each index of `snode`. The reference program is written for one: setup_inputs(seed, part) draws one part's arguments, and reference() takes and returns one part's arrays. A program takes and returns all parts, laid end to end along the dimension named above; each array names one. Nothing has to cross between parts.
Inputs may be any that keep to these rules, and one draw needn't show every extreme that they name: Tile (i, j) takes part exactly where fill_mask is 1; diagonal tiles are always 1. `block_order`: each row is a permutation of the 80 ancestor blocks.
All inputs are finite; a program needn't handle non-finite values.
Results may differ from the reference program's by a relative error of at most 0.014.
Values may be sent and summed in bfloat16 or wider, within the bound.
No kernel may reach another device: no remote copies, remote signals or barrier semaphores. Data moves between devices by JAX's collectives and lax.ppermute only.
A program may use at most 128 MiB of HBM per device.

```python
import jax
import jax.numpy as jnp
from jax import lax

TILE = 256
BLOCKS = 80
SNODES = 2
ORDER = 20480


def draw_fill_mask(key, part):
    sub_key = jax.random.fold_in(key, 11)
    row_ids = jnp.arange(BLOCKS, dtype=jnp.int32)[:, None]
    col_ids = jnp.arange(BLOCKS, dtype=jnp.int32)[None, :]
    threshold = 20 + 80 * row_ids // (BLOCKS - 1)
    drawn_value = jax.random.randint(sub_key, (BLOCKS, BLOCKS), 0, 100)
    filled = jnp.where(drawn_value < threshold, 1, 0)
    return jnp.where(row_ids == col_ids, 1, filled).astype(jnp.int32)


def levels(rng, shape, split, smallest, top_value):
    factor_of = 1.0
    for position, blocks in split:
        heights = jax.random.uniform(jax.random.fold_in(jax.random.fold_in(rng, 6), position), (blocks,), jnp.float32, smallest / len(split), top_value / len(split))
        factor_of = factor_of * jnp.repeat(jnp.exp(heights), shape[position] // blocks).reshape((-1,) + (1,) * (len(shape) - 1 - position))
    return factor_of


def gaussian(stream_key, dims, width, reach, cuts=(), held_as=jnp.bfloat16):
    loudness = levels(stream_key, dims, cuts, -0.22, 0.18) if cuts else 1.0
    drawn = jax.random.normal(stream_key, dims, jnp.float32) * width * loudness
    return jnp.minimum(jnp.maximum(drawn, -reach), reach).astype(held_as)


def setup_inputs(seed: int = 0, part: int = 0) -> dict:
    keys = jax.random.split(jax.random.key(seed), 6)
    part_splits = jax.random.split(jax.random.fold_in(keys[5], part), 6)
    ancestor_inverse = gaussian(part_splits[0], (ORDER, ORDER), 1.3, 8.0, ((0, 16), (1, 8)))
    fill_mask = draw_fill_mask(jax.random.fold_in(jax.random.fold_in(keys[5], part), 71), part)
    block_order = jax.vmap(lambda own: jax.random.permutation(own, BLOCKS))(jax.random.split(part_splits[2], SNODES)).reshape((SNODES, BLOCKS)).astype(jnp.int32)
    l_rows = gaussian(part_splits[3], (SNODES, ORDER, TILE), 1.0, 6.0, ((1, 128),))
    diag_inverse = gaussian(part_splits[4], (SNODES, TILE, TILE), (BLOCKS * TILE * TILE) ** -0.5, 0.0024414062)
    return dict(ancestor_inverse=ancestor_inverse, fill_mask=fill_mask, block_order=block_order, l_rows=l_rows, diag_inverse=diag_inverse)


def reference(ancestor_inverse, fill_mask, block_order, l_rows, diag_inverse):
    snode_count = diag_inverse.shape[0]
    tile_size = diag_inverse.shape[1]
    block_count = fill_mask.shape[0]
    normed = jnp.einsum("sxy,syz->sxz", l_rows.astype(jnp.float32), diag_inverse.astype(jnp.float32), precision=lax.Precision.HIGHEST).astype(jnp.bfloat16)
    pieces = normed.reshape(snode_count, block_count, tile_size, tile_size).astype(jnp.float32)
    targets = jnp.arange(block_count, dtype=jnp.int32)
    selector = (block_order[:, None, :] == targets[None, :, None]).astype(jnp.float32)
    aligned = jnp.einsum("saq,sqxy->saxy", selector, pieces, precision=lax.Precision.HIGHEST)
    stacked = aligned.transpose(1, 2, 0, 3).reshape(block_count * tile_size, snode_count * tile_size)

    def one_row(block_id):
        row_slab = lax.dynamic_slice_in_dim(ancestor_inverse, block_id * tile_size, tile_size, 0).astype(jnp.float32)
        row_gate = jnp.repeat(lax.dynamic_slice_in_dim(fill_mask, block_id, 1, 0)[0].astype(jnp.float32), tile_size)
        return -jnp.dot(row_slab * row_gate[None, :], stacked, precision=lax.Precision.HIGHEST)

    product = lax.map(one_row, jnp.arange(block_count, dtype=jnp.int32))
    product = product.reshape(block_count * tile_size, snode_count, tile_size)
    return product.transpose(1, 2, 0).astype(jnp.bfloat16)
```

```python
import functools

import jax
import jax.numpy as jnp
from jax import lax
from jax.experimental import pallas as pl
from jax.experimental.pallas import tpu as pltpu
from jax.sharding import PartitionSpec as P

NX, NZ = 4, 4
VMEM = pltpu.VMEM
SMEM = pltpu.SMEM
SLICE = 16


def whole(space=VMEM):
    return pl.BlockSpec(memory_space=space)


def params():
    return pltpu.CompilerParams(vmem_limit_bytes=48 * 1024 * 1024)


def spread_kernel(pos_ref, l_ref, out_ref):
    rows = out_ref.shape[0]
    first = pos_ref[0] + pos_ref[1] * (l_ref.shape[1] // SLICE)
    for i in range(l_ref.shape[1] // SLICE):
        slot = lax.rem(first + i, rows)
        for s in range(l_ref.shape[0]):
            out_ref[slot, s] = l_ref[s, i * SLICE : (i + 1) * SLICE]


def compact_kernel(pos_ref, got_ref, out_ref):
    rows = got_ref.shape[0]
    count = out_ref.shape[1]
    first = pos_ref[0] - pos_ref[1] * count + 16 * rows
    for i in range(count):
        slot = lax.rem(first - i, rows)
        for copy in range(out_ref.shape[0]):
            out_ref[copy, i] = got_ref[slot]


def select_kernel(pos_ref, order_ref, all_ref, diag_ref, out_ref, from_ref, picked):
    snodes, blocks = order_ref.shape
    rows = 16
    per_row = blocks // rows
    share = out_ref.shape[0] // SLICE
    tile = diag_ref.shape[1]

    def step(q, carry):
        group = q // per_row
        k = lax.rem(pos_ref[0] - group + rows, rows)
        place = (q - group * per_row) * rows + k
        for s in range(snodes):
            a = order_ref[s, q] - pos_ref[1] * share

            @pl.when((a >= 0) & (a < share))
            def _():
                picked[s, pl.ds(pl.multiple_of(a * SLICE, SLICE), SLICE), :] = all_ref[place, s]
                from_ref[s, a] = group

        return carry

    lax.fori_loop(0, blocks, step, 0)
    for s in range(snodes):
        out_ref[:, s * tile : (s + 1) * tile] = jnp.dot(
            picked[s], diag_ref[s], preferred_element_type=jnp.float32
        ).astype(out_ref.dtype)


def product_kernel(pos_ref, from_ref, mask_ref, a_ref, o_ref, u_ref, d_ref, fu_ref, fd_ref, out_ref, stacked, *, zshift):
    i = pl.program_id(0)
    rows = 16
    share = stacked.shape[0] // (rows * SLICE)
    tile = rows * SLICE
    x, z = pos_ref[2], pos_ref[3]
    block = share * SLICE

    @pl.when(i == 0)
    def _():
        pieces = []
        for xs, ref, base in ((0, o_ref, 0), (-1, u_ref, 0), (1, d_ref, 0)):
            for n, zs in enumerate(zshift):
                pieces.append((xs, zs, ref, n * block))
        half = len(zshift) // 2
        for n, zs in enumerate(zshift):
            pieces.append((2, zs, fu_ref, n * block) if n < half else (2, zs, fd_ref, (n - half) * block))
        for s in range(from_ref.shape[0]):
            for a in range(share):
                group = from_ref[s, a]
                for xs, zs, ref, base in pieces:
                    j = lax.rem(x + xs + NX, NX) * NZ + lax.rem(z + zs + NZ, NZ)
                    k = lax.rem(j - group + rows, rows)
                    stacked[
                        pl.ds(pl.multiple_of(a * tile + k * SLICE, SLICE), SLICE), s * tile : (s + 1) * tile
                    ] = ref[base + a * SLICE : base + (a + 1) * SLICE, s * tile : (s + 1) * tile]

    gates = []
    for j in range(share):
        gate = mask_ref[pos_ref[0] * pl.num_programs(0) + i, pos_ref[1] * share + j]
        keep = jnp.full((1, tile), gate, jnp.int32).astype(jnp.float32)
        gates.append(keep.astype(jnp.bfloat16))
    gate_row = jnp.concatenate(gates, axis=1)
    out_ref[...] = (
        -jnp.dot(a_ref[...] * gate_row, stacked[...], preferred_element_type=jnp.float32)
    ).astype(out_ref.dtype)


def ring(value, axis, up, down):
    half = value.shape[0] // 2
    from_up = lax.ppermute(value, axis, up)
    from_down = lax.ppermute(value, axis, down)
    far_up = lax.ppermute(from_up[:half], axis, up)
    far_down = lax.ppermute(from_down[half:], axis, down)
    return from_up, from_down, far_up, far_down


def per_device(ancestor_inverse, fill_mask, block_order, l_rows, diag_inverse):
    rows, cols = lax.axis_size("row"), lax.axis_size("col")
    row_index, col_index = lax.axis_index("row"), lax.axis_index("col")
    snodes, tile = diag_inverse.shape[0], diag_inverse.shape[1]
    local_rows, local_cols = ancestor_inverse.shape
    count = l_rows.shape[1] // SLICE
    blocks = block_order.shape[1]
    share = blocks // cols
    bf16 = jnp.bfloat16
    pos = jnp.stack([row_index, col_index, row_index // NZ, row_index % NZ]).astype(jnp.int32)

    spread = pl.pallas_call(
        spread_kernel,
        out_shape=jax.ShapeDtypeStruct((rows, snodes, SLICE, tile), bf16),
        in_specs=[whole(SMEM), whole()],
        out_specs=whole(),
        compiler_params=params(),
        name="spread",
    )(pos, l_rows)
    got = lax.all_to_all(spread, "row", 0, 0, tiled=True)
    copies = pl.pallas_call(
        compact_kernel,
        out_shape=jax.ShapeDtypeStruct((cols, count, snodes, SLICE, tile), bf16),
        in_specs=[whole(SMEM), whole()],
        out_specs=whole(),
        compiler_params=params(),
        name="compact",
    )(pos, got)
    everything = lax.all_to_all(copies, "col", 0, 0, tiled=True)
    everything = everything.reshape(cols * count, snodes, SLICE, tile)
    own, source = pl.pallas_call(
        select_kernel,
        out_shape=(
            jax.ShapeDtypeStruct((share * SLICE, snodes * tile), bf16),
            jax.ShapeDtypeStruct((snodes, share), jnp.int32),
        ),
        in_specs=[whole(SMEM), whole(SMEM), whole(), whole()],
        out_specs=(whole(), whole(SMEM)),
        scratch_shapes=[VMEM((snodes, share * SLICE, tile), bf16)],
        compiler_params=params(),
        name="select",
    )(pos, block_order, everything, diag_inverse)

    def shift(dx, dz):
        return [(r, ((r // NZ + dx) % NX) * NZ + (r % NZ + dz) % NZ) for r in range(rows)]

    up, down, far_up, far_down = ring(own, "row", shift(0, 1), shift(0, -1))
    plane = jnp.concatenate([own, up, down, far_up, far_down], axis=0)
    xu, xd, xfu, xfd = ring(plane, "row", shift(1, 0), shift(-1, 0))

    row_blocks = local_rows // tile
    partial_value = pl.pallas_call(
        functools.partial(product_kernel, zshift=(0, -1, 1, 2)),
        out_shape=jax.ShapeDtypeStruct((local_rows, snodes * tile), bf16),
        grid=(row_blocks,),
        in_specs=[whole(SMEM), whole(SMEM), whole(SMEM), pl.BlockSpec((tile, local_cols), lambda i: (i, 0))]
        + [whole()] * 5,
        out_specs=pl.BlockSpec((tile, snodes * tile), lambda i: (i, 0)),
        scratch_shapes=[VMEM((local_cols, snodes * tile), bf16)],
        compiler_params=params(),
        name="product",
    )(pos, source, fill_mask, ancestor_inverse, plane, xu, xd, xfu, xfd)

    share_rows = local_rows // cols
    shares = lax.all_to_all(partial_value, "col", 0, 0, tiled=True)
    summed = shares.reshape(cols, share_rows, snodes, tile).astype(jnp.float32).sum(0)
    return summed.transpose(1, 2, 0).astype(bf16)


def solution(mesh):
    return jax.shard_map(
        per_device,
        mesh=mesh,
        in_specs=(
            P(("snode", "row"), "col"),
            P("snode", None),
            P("snode", None),
            P("snode", ("row", "col"), None),
            P("snode", None, None),
        ),
        out_specs=P("snode", None, ("row", "col")),
        check_vma=False,
    )
```

```python
import jax
import jax.numpy as jnp
from jax import lax
from jax.experimental import pallas as pl
from jax.experimental.pallas import tpu as pltpu
from jax.sharding import Mesh
from jax.sharding import PartitionSpec as P

NX, NZ, NL, NY = 4, 4, 2, 4
SLICE = 16
LANES = 128
VMEM = pltpu.VMEM
SMEM = pltpu.SMEM


def whole(space=VMEM):
    return pl.BlockSpec(memory_space=space)


def params():
    return pltpu.CompilerParams(vmem_limit_bytes=48 * 1024 * 1024)


def spread_kernel(pos_ref, l_ref, out_ref):
    snodes, rows, _ = l_ref.shape
    count = rows // SLICE
    first = (pos_ref[2] * NY + pos_ref[3]) * count
    for i in range(count):
        k = (first + i) & (NX * NY - 1)
        for l in range(NL):
            slot = ((k // NY) * NL + l) * NY + (k & (NY - 1))
            for s in range(snodes):
                out_ref[slot, s] = l_ref[s, i * SLICE : (i + 1) * SLICE, l * LANES : (l + 1) * LANES]


def compact_kernel(pos_ref, got_ref, out_ref):
    snodes = got_ref.shape[1]
    per_row = out_ref.shape[0] // (NX * snodes)
    count = per_row * NX * NY // (NL * NY)
    k = pos_ref[0] * NY + pos_ref[3]
    for t in range(per_row):
        col = (t * NX * NY + k) // count
        for x in range(NX):
            for s in range(snodes):
                out_ref[(x * per_row + t) * snodes + s] = got_ref[x * NL * NY + col, s]


def route_kernel(pos_ref, order_ref, all_ref, out_ref):
    snodes, blocks = order_ref.shape
    per_row = blocks // (NX * NZ)
    part = NX * per_row * snodes
    for z in range(NZ):
        d = (z - pos_ref[1]) & (NZ - 1)
        base = jnp.where(d == 0, 0, jnp.where(d == 3, 1, jnp.where(d == 1, 2, 3))) * part
        for x in range(NX):
            for t in range(per_row):
                q = (x * NZ + z) * per_row + t
                for s in range(snodes):
                    out_ref[order_ref[s, q], s] = all_ref[base + (x * per_row + t) * snodes + s]


def normal_kernel(got_ref, diag_ref, out_ref, picked):
    _, share, snodes = got_ref.shape[:3]
    tile = diag_ref.shape[1]
    for s in range(snodes):
        for a in range(share):
            for y in range(NY):
                at = (a * NY + y) * SLICE
                for l in range(NL):
                    picked[at : at + SLICE, l * LANES : (l + 1) * LANES] = got_ref[l * NY + y, a, s]
        out_ref[:, s * tile : (s + 1) * tile] = jnp.dot(
            picked[...], diag_ref[s], preferred_element_type=jnp.float32
        ).astype(out_ref.dtype)


def product_kernel(pos_ref, mask_ref, a_ref, o_ref, u_ref, d_ref, fu_ref, fd_ref, out_ref, stacked):
    i = pl.program_id(0)
    quarter = NY * SLICE
    tile = NX * quarter
    share = stacked.shape[0] // tile

    @pl.when(i == 0)
    def _():
        for a in range(share):
            far, at = (fu_ref, a) if a < share // 2 else (fd_ref, a - share // 2)
            for shift, ref, n in ((0, o_ref, a), (-1, u_ref, a), (1, d_ref, a), (2, far, at)):
                x = (pos_ref[0] + shift) & (NX - 1)
                stacked[pl.ds(pl.multiple_of(a * tile + x * quarter, quarter), quarter), :] = ref[
                    n * quarter : (n + 1) * quarter, :
                ]

    gates = []
    row = (pos_ref[0] * NZ + pos_ref[1]) * pl.num_programs(0) + i
    col = (pos_ref[2] * NY + pos_ref[3]) * share
    for j in range(share):
        keep = jnp.full((1, tile), mask_ref[row, col + j], jnp.int32).astype(jnp.float32)
        gates.append(keep.astype(jnp.bfloat16))
    gate_row = jnp.concatenate(gates, axis=1)
    out_ref[...] = (
        -jnp.dot(a_ref[...] * gate_row, stacked[...], preferred_element_type=jnp.float32)
    ).astype(out_ref.dtype)


def ring(value, axis):
    size = lax.axis_size(axis)
    up = [(i, (i + 1) % size) for i in range(size)]
    down = [(i, (i - 1) % size) for i in range(size)]
    half = value.shape[0] // 2
    from_up = lax.ppermute(value, axis, up)
    from_down = lax.ppermute(value, axis, down)
    far_up = lax.ppermute(from_up[:half], axis, up)
    far_down = lax.ppermute(from_down[half:], axis, down)
    return value, from_up, from_down, far_up, far_down


def per_device(ancestor_inverse, fill_mask, block_order, l_rows, diag_inverse):
    snodes, tile = diag_inverse.shape[0], diag_inverse.shape[1]
    local_rows, local_cols = ancestor_inverse.shape
    blocks = block_order.shape[1]
    cols = NL * NY
    share = blocks // cols
    width = snodes * tile
    bf16 = jnp.bfloat16
    pos = jnp.stack([lax.axis_index(name) for name in ("x", "z", "l", "y")]).astype(jnp.int32)

    spread = pl.pallas_call(
        spread_kernel,
        out_shape=jax.ShapeDtypeStruct((NX * cols, snodes, SLICE, LANES), bf16),
        in_specs=[whole(SMEM), whole()],
        out_specs=whole(),
        compiler_params=params(),
        name="spread",
    )(pos, l_rows)
    got = lax.all_to_all(spread, ("x", "l", "y"), 0, 0, tiled=True)
    mine = pl.pallas_call(
        compact_kernel,
        out_shape=jax.ShapeDtypeStruct((blocks // NZ * snodes, SLICE, LANES), bf16),
        in_specs=[whole(SMEM), whole()],
        out_specs=whole(),
        compiler_params=params(),
        name="compact",
    )(pos, got)
    everything = jnp.concatenate(ring(mine, "z"), axis=0)
    routed = pl.pallas_call(
        route_kernel,
        out_shape=jax.ShapeDtypeStruct((blocks, snodes, SLICE, LANES), bf16),
        in_specs=[whole(SMEM), whole(SMEM), whole()],
        out_specs=whole(),
        compiler_params=params(),
        name="route",
    )(pos, block_order, everything)
    quarters = lax.all_to_all(routed, ("l", "y"), 0, 0, tiled=True)
    own = pl.pallas_call(
        normal_kernel,
        out_shape=jax.ShapeDtypeStruct((share * NY * SLICE, width), bf16),
        in_specs=[whole(), whole()],
        out_specs=whole(),
        scratch_shapes=[VMEM((share * NY * SLICE, tile), bf16)],
        compiler_params=params(),
        name="normal",
    )(quarters.reshape(cols, share, snodes, SLICE, LANES), diag_inverse)
    partial_value = pl.pallas_call(
        product_kernel,
        out_shape=jax.ShapeDtypeStruct((local_rows, width), bf16),
        grid=(local_rows // tile,),
        in_specs=[whole(SMEM), whole(SMEM), pl.BlockSpec((tile, local_cols), lambda i: (i, 0))] + [whole()] * 5,
        out_specs=pl.BlockSpec((tile, width), lambda i: (i, 0)),
        scratch_shapes=[VMEM((local_cols, width), bf16)],
        compiler_params=params(),
        name="product",
    )(pos, fill_mask, ancestor_inverse, *ring(own, "x"))
    share_rows = local_rows // cols
    shares = lax.all_to_all(partial_value, ("l", "y"), 0, 0, tiled=True)
    summed = shares.reshape(cols, share_rows, snodes, tile).astype(jnp.float32).sum(0)
    return summed.transpose(1, 2, 0).astype(bf16)


def solution(mesh):
    fine = Mesh(
        mesh.devices.reshape(NX, NZ, NL, NY, mesh.shape["snode"]), ("x", "z", "l", "y", "snode")
    )
    row, col = ("x", "z"), ("l", "y")
    return jax.shard_map(
        per_device,
        mesh=fine,
        in_specs=(
            P(("snode", *row), col),
            P("snode", None),
            P("snode", None),
            P("snode", (*row, *col), None),
            P("snode", None, None),
        ),
        out_specs=P("snode", None, (*row, *col)),
        check_vma=False,
    )
```

```python
import functools

import jax
import jax.numpy as jnp
from jax import lax
from jax.experimental import pallas as pl
from jax.experimental.pallas import tpu as pltpu
from jax.sharding import Mesh
from jax.sharding import PartitionSpec as P

NX, NZ, NL, NY = 4, 4, 2, 4
SLICE = 16
LANES = 128
VMEM = pltpu.VMEM
SMEM = pltpu.SMEM


def whole(space=VMEM):
    return pl.BlockSpec(memory_space=space)


def params():
    return pltpu.CompilerParams(vmem_limit_bytes=24 * 1024 * 1024)


def place_of(x):
    return ((x & 1) * 2 + x // 2) * NY


def spread_kernel(pos_ref, l_ref, out_ref):
    snodes, rows, _ = l_ref.shape
    count = rows // SLICE
    first = (pos_ref[2] * NY + pos_ref[3]) * count
    for i in range(count):
        k = (first + i) & (NX * NY - 1)
        for l in range(NL):
            x = ((k // NY) & 1) * 2 + k // (2 * NY)
            slot = (x * NL + l) * NY + (k & (NY - 1))
            for s in range(snodes):
                out_ref[slot, s] = l_ref[s, i * SLICE : (i + 1) * SLICE, l * LANES : (l + 1) * LANES]


def compact_kernel(pos_ref, got_ref, out_ref):
    snodes = got_ref.shape[1]
    per_row = out_ref.shape[0] // (NX * snodes)
    count = per_row * NX * NY // (NL * NY)
    k = place_of(pos_ref[0]) + pos_ref[3]
    for t in range(per_row):
        col = (t * NX * NY + k) // count
        for x in range(NX):
            for s in range(snodes):
                out_ref[(x * per_row + t) * snodes + s] = got_ref[x * NL * NY + col, s]


def route_kernel(pos_ref, order_ref, all_ref, out_ref):
    snodes, blocks = order_ref.shape
    per_row = blocks // (NX * NZ)
    part = NX * per_row * snodes
    for z in range(NZ):
        d = (z - pos_ref[1]) & (NZ - 1)
        base = jnp.where(d == 0, 0, jnp.where(d == 3, 1, jnp.where(d == 1, 2, 3))) * part
        for x in range(NX):
            for t in range(per_row):
                q = (x * NZ + z) * per_row + t
                for s in range(snodes):
                    out_ref[order_ref[s, q], s] = all_ref[base + (x * per_row + t) * snodes + s]


def normal_kernel(got_ref, diag_ref, out_ref, picked):
    _, share, snodes = got_ref.shape[:3]
    tile = diag_ref.shape[1]
    for s in range(snodes):
        for a in range(share):
            for y in range(NY):
                at = (a * NY + y) * SLICE
                for l in range(NL):
                    picked[at : at + SLICE, l * LANES : (l + 1) * LANES] = got_ref[l * NY + y, a, s]
        out_ref[:, s * tile : (s + 1) * tile] = jnp.dot(
            picked[...], diag_ref[s], preferred_element_type=jnp.float32
        ).astype(out_ref.dtype)


def fill(stacked, pairs):
    quarter = NY * SLICE
    share = stacked.shape[0] // (2 * quarter)
    for x, refs in pairs:
        each = share // len(refs)
        for a in range(share):
            at = pl.multiple_of(a * 2 * quarter + (x // 2) * quarter, quarter)
            n = a % each
            stacked[pl.ds(at, quarter), :] = refs[a // each][n * quarter : (n + 1) * quarter, :]


def gate_kernel(own_half, pos_ref, mask_ref, a_ref, _after, out_ref, arrived):
    rows, half = out_ref.shape
    share = half // LANES
    tile = 2 * LANES
    x = pos_ref[0]
    side = (x & 1) if own_half else 1 - (x & 1)
    copies = []
    for a in range(share):
        columns = pl.ds(pl.multiple_of(a * tile + side * LANES, LANES), LANES)
        copies.append(
            pltpu.make_async_copy(a_ref.at[:, columns], out_ref.at[:, a * LANES : (a + 1) * LANES], arrived.at[a])
        )
        copies[a].start()
    row = (x * NZ + pos_ref[1]) * (rows // tile)
    col = (pos_ref[2] * NY + pos_ref[3]) * share
    for a in range(share):
        copies[a].wait()
        at = slice(a * LANES, (a + 1) * LANES)
        for i in range(rows // tile):
            keep = jnp.full((1, LANES), mask_ref[row + i, col + a], jnp.int32).astype(jnp.float32)
            down = slice(i * tile, (i + 1) * tile)
            out_ref[down, at] = out_ref[down, at] * keep.astype(jnp.bfloat16)


def near_kernel(pos_ref, a_ref, ul_ref, uh_ref, dl_ref, dh_ref, out_ref, stacked):
    x = pos_ref[0]
    fill(stacked, (((x - 1) & (NX - 1), (ul_ref, uh_ref)), ((x + 1) & (NX - 1), (dl_ref, dh_ref))))
    tile = 2 * LANES
    for n in range(out_ref.shape[1] // tile):
        at = slice(n * tile, (n + 1) * tile)
        out_ref[:, at] = jnp.dot(a_ref[...], stacked[:, at], preferred_element_type=jnp.float32)


def far_kernel(pos_ref, a_ref, near_ref, own_ref, fu_ref, fd_ref, out_ref, stacked):
    x = pos_ref[0]
    fill(stacked, ((x, (own_ref,)), ((x + 2) & (NX - 1), (fu_ref, fd_ref))))
    tile = 2 * LANES
    for n in range(out_ref.shape[1] // tile):
        at = slice(n * tile, (n + 1) * tile)
        out_ref[:, at] = (
            -(near_ref[:, at] + jnp.dot(a_ref[...], stacked[:, at], preferred_element_type=jnp.float32))
        ).astype(out_ref.dtype)


def ring(value, axis):
    size = lax.axis_size(axis)
    up = [(i, (i + 1) % size) for i in range(size)]
    down = [(i, (i - 1) % size) for i in range(size)]
    half = value.shape[0] // 2
    from_up = lax.ppermute(value, axis, up)
    from_down = lax.ppermute(value, axis, down)
    far_up = lax.ppermute(from_up[:half], axis, up)
    far_down = lax.ppermute(from_down[half:], axis, down)
    return value, from_up, from_down, far_up, far_down


def split_ring(value, axis, beside):
    size = lax.axis_size(axis)
    up = [(i, (i + 1) % size) for i in range(size)]
    down = [(i, (i - 1) % size) for i in range(size)]
    half = value.shape[0] // 2
    low, high = value[:half], value[half:]
    up_low = lax.ppermute(low, axis, up)
    down_high = lax.ppermute(high, axis, down)
    up_high = lax.ppermute(high, axis, up)
    down_low = lax.ppermute(low, axis, down)
    up_low, down_high, made = lax.optimization_barrier((up_low, down_high, beside()))
    far_up = lax.ppermute(up_low, axis, up)
    far_down = lax.ppermute(down_high, axis, down)
    return (value, up_low, up_high, down_low, down_high, far_up, far_down), made


def per_device(ancestor_inverse, fill_mask, block_order, l_rows, diag_inverse):
    snodes, tile = diag_inverse.shape[0], diag_inverse.shape[1]
    local_rows, local_cols = ancestor_inverse.shape
    blocks = block_order.shape[1]
    cols = NL * NY
    share = blocks // cols
    width = snodes * tile
    bf16 = jnp.bfloat16
    pos = jnp.stack([lax.axis_index(name) for name in ("x", "z", "l", "y")]).astype(jnp.int32)

    spread = pl.pallas_call(
        spread_kernel,
        out_shape=jax.ShapeDtypeStruct((NX * cols, snodes, SLICE, LANES), bf16),
        in_specs=[whole(SMEM), whole()],
        out_specs=whole(),
        compiler_params=params(),
        name="spread",
    )(pos, l_rows)
    got = lax.all_to_all(spread, ("x", "l", "y"), 0, 0, tiled=True)
    mine = pl.pallas_call(
        compact_kernel,
        out_shape=jax.ShapeDtypeStruct((blocks // NZ * snodes, SLICE, LANES), bf16),
        in_specs=[whole(SMEM), whole()],
        out_specs=whole(),
        compiler_params=params(),
        name="compact",
    )(pos, got)
    half_cols = local_cols // 2

    def gate(own_half, after):
        return pl.pallas_call(
            functools.partial(gate_kernel, own_half),
            out_shape=jax.ShapeDtypeStruct((local_rows, half_cols), bf16),
            in_specs=[whole(SMEM), whole(SMEM), whole(pl.ANY), whole(pl.ANY)],
            out_specs=whole(),
            scratch_shapes=[pltpu.SemaphoreType.DMA((share,))],
            compiler_params=params(),
            cost_estimate=pl.CostEstimate(
                flops=local_rows * half_cols, bytes_accessed=4 * local_rows * half_cols, transcendentals=0
            ),
            name="gate",
        )(pos, fill_mask, ancestor_inverse, after)

    everything = jnp.concatenate(ring(mine, "z"), axis=0)
    routed = pl.pallas_call(
        route_kernel,
        out_shape=jax.ShapeDtypeStruct((blocks, snodes, SLICE, LANES), bf16),
        in_specs=[whole(SMEM), whole(SMEM), whole()],
        out_specs=whole(),
        compiler_params=params(),
        name="route",
    )(pos, block_order, everything)
    quarters = lax.all_to_all(routed, ("l", "y"), 0, 0, tiled=True)
    own = pl.pallas_call(
        normal_kernel,
        out_shape=jax.ShapeDtypeStruct((share * NY * SLICE, width), bf16),
        in_specs=[whole(), whole()],
        out_specs=whole(),
        scratch_shapes=[VMEM((share * NY * SLICE, tile), bf16)],
        compiler_params=params(),
        name="normal",
    )(quarters.reshape(cols, share, snodes, SLICE, LANES), diag_inverse)
    (own, *near, far_up, far_down), gated_own = split_ring(own, "x", lambda: gate(True, own))
    gated_other = gate(False, own)
    near_value = pl.pallas_call(
        near_kernel,
        out_shape=jax.ShapeDtypeStruct((local_rows, width), jnp.float32),
        in_specs=[whole(SMEM)] + [whole()] * 5,
        out_specs=whole(),
        scratch_shapes=[VMEM((half_cols, width), bf16)],
        compiler_params=params(),
        cost_estimate=pl.CostEstimate(
            flops=local_rows * local_cols * width, bytes_accessed=0, transcendentals=0
        ),
        name="near",
    )(pos, gated_other, *near)
    partial_value = pl.pallas_call(
        far_kernel,
        out_shape=jax.ShapeDtypeStruct((local_rows, width), bf16),
        in_specs=[whole(SMEM)] + [whole()] * 5,
        out_specs=whole(),
        scratch_shapes=[VMEM((half_cols, width), bf16)],
        compiler_params=params(),
        name="far",
    )(pos, gated_own, near_value, own, far_up, far_down)
    share_rows = local_rows // cols
    shares = lax.all_to_all(partial_value, ("l", "y"), 0, 0, tiled=True)
    summed = shares.reshape(cols, share_rows, snodes, tile).astype(jnp.float32).sum(0)
    return summed.transpose(1, 2, 0).astype(bf16)


def solution(mesh):
    fine = Mesh(
        mesh.devices.reshape(NX, NZ, NL, NY, mesh.shape["snode"]), ("x", "z", "l", "y", "snode")
    )
    row, col = ("x", "z"), ("l", "y")
    return jax.shard_map(
        per_device,
        mesh=fine,
        in_specs=(
            P(("snode", *row), col),
            P("snode", None),
            P("snode", None),
            P("snode", (*row, *col), None),
            P("snode", None, None),
        ),
        out_specs=P("snode", None, (*row, *col)),
        check_vma=False,
    )
```

```python
import functools

import jax
import jax.numpy as jnp
from jax import lax
from jax.experimental import pallas as pl
from jax.experimental.pallas import tpu as pltpu
from jax.sharding import Mesh
from jax.sharding import PartitionSpec as P

NX, NZ, NL, NY = 4, 4, 2, 4
SLICE = 16
LANES = 128
VMEM = pltpu.VMEM
SMEM = pltpu.SMEM


def whole(space=VMEM):
    return pl.BlockSpec(memory_space=space)


def params():
    return pltpu.CompilerParams(vmem_limit_bytes=24 * 1024 * 1024)


def place_of(x):
    return ((x & 1) * 2 + x // 2) * NY


def spread_kernel(pos_ref, l_ref, out_ref):
    snodes, rows, _ = l_ref.shape
    count = rows // SLICE
    first = (pos_ref[2] * NY + pos_ref[3]) * count
    for i in range(count):
        k = (first + i) & (NX * NY - 1)
        for l in range(NL):
            x = ((k // NY) & 1) * 2 + k // (2 * NY)
            slot = (x * NL + l) * NY + (k & (NY - 1))
            for s in range(snodes):
                out_ref[slot, s] = l_ref[s, i * SLICE : (i + 1) * SLICE, l * LANES : (l + 1) * LANES]


def compact_kernel(pos_ref, _order, got_ref, out_ref):
    snodes = got_ref.shape[1]
    per_row = out_ref.shape[0] // (NX * snodes)
    count = per_row * NX * NY // (NL * NY)
    k = place_of(pos_ref[0]) + pos_ref[3]
    for t in range(per_row):
        col = (t * NX * NY + k) // count
        for x in range(NX):
            for s in range(snodes):
                out_ref[(x * per_row + t) * snodes + s] = got_ref[x * NL * NY + col, s]


def route_kernel(pos_ref, order_ref, all_ref, out_ref):
    snodes, blocks = order_ref.shape
    per_row = blocks // (NX * NZ)
    part = NX * per_row * snodes
    for z in range(NZ):
        d = (z - pos_ref[1]) & (NZ - 1)
        base = jnp.where(d == 0, 0, jnp.where(d == 3, 1, jnp.where(d == 1, 2, 3))) * part
        for x in range(NX):
            for t in range(per_row):
                q = (x * NZ + z) * per_row + t
                for s in range(snodes):
                    out_ref[order_ref[s, q], s] = all_ref[base + (x * per_row + t) * snodes + s]


def normal_kernel(got_ref, diag_ref, out_ref, picked):
    _, share, snodes = got_ref.shape[:3]
    tile = diag_ref.shape[1]
    for s in range(snodes):
        for a in range(share):
            for y in range(NY):
                at = (a * NY + y) * SLICE
                for l in range(NL):
                    picked[at : at + SLICE, l * LANES : (l + 1) * LANES] = got_ref[l * NY + y, a, s]
        out_ref[:, s * tile : (s + 1) * tile] = jnp.dot(
            picked[...], diag_ref[s], preferred_element_type=jnp.float32
        ).astype(out_ref.dtype)


def fill(stacked, pairs):
    quarter = NY * SLICE
    share = stacked.shape[0] // (2 * quarter)
    for x, refs in pairs:
        each = share // len(refs)
        for a in range(share):
            at = pl.multiple_of(a * 2 * quarter + (x // 2) * quarter, quarter)
            n = a % each
            stacked[pl.ds(at, quarter), :] = refs[a // each][n * quarter : (n + 1) * quarter, :]


def gate_kernel(own_half, pos_ref, mask_ref, a_ref, _after, out_ref, arrived):
    rows, half = out_ref.shape
    share = half // LANES
    tile = 2 * LANES
    x = pos_ref[0]
    side = (x & 1) if own_half else 1 - (x & 1)
    copies = []
    for a in range(share):
        columns = pl.ds(pl.multiple_of(a * tile + side * LANES, LANES), LANES)
        copies.append(
            pltpu.make_async_copy(a_ref.at[:, columns], out_ref.at[:, a * LANES : (a + 1) * LANES], arrived.at[a])
        )
        copies[a].start()
    row = (x * NZ + pos_ref[1]) * (rows // tile)
    col = (pos_ref[2] * NY + pos_ref[3]) * share
    for a in range(share):
        copies[a].wait()
        at = slice(a * LANES, (a + 1) * LANES)
        for i in range(rows // tile):
            keep = jnp.full((1, LANES), mask_ref[row + i, col + a], jnp.int32).astype(jnp.float32)
            down = slice(i * tile, (i + 1) * tile)
            out_ref[down, at] = out_ref[down, at] * keep.astype(jnp.bfloat16)


def near_kernel(pos_ref, a_ref, own_ref, ul_ref, uh_ref, dl_ref, dh_ref, out_ref, begun_ref, stacked):
    x = pos_ref[0]
    fill(begun_ref, ((x, (own_ref,)),))
    fill(stacked, (((x - 1) & (NX - 1), (ul_ref, uh_ref)), ((x + 1) & (NX - 1), (dl_ref, dh_ref))))
    tile = 2 * LANES
    for n in range(out_ref.shape[1] // tile):
        at = slice(n * tile, (n + 1) * tile)
        out_ref[:, at] = jnp.dot(a_ref[...], stacked[:, at], preferred_element_type=jnp.float32)


def far_kernel(pos_ref, a_ref, near_ref, _, fu_ref, fd_ref, out_ref, stacked):
    x = pos_ref[0]
    fill(stacked, (((x + 2) & (NX - 1), (fu_ref, fd_ref)),))
    tile = 2 * LANES
    for n in range(out_ref.shape[1] // tile):
        at = slice(n * tile, (n + 1) * tile)
        out_ref[:, at] = (
            -(near_ref[:, at] + jnp.dot(a_ref[...], stacked[:, at], preferred_element_type=jnp.float32))
        ).astype(out_ref.dtype)


def ring(value, axis):
    size = lax.axis_size(axis)
    up = [(i, (i + 1) % size) for i in range(size)]
    down = [(i, (i - 1) % size) for i in range(size)]
    half = value.shape[0] // 2
    from_up = lax.ppermute(value, axis, up)
    from_down = lax.ppermute(value, axis, down)
    far_up = lax.ppermute(from_up[:half], axis, up)
    far_down = lax.ppermute(from_down[half:], axis, down)
    return value, from_up, from_down, far_up, far_down


def split_ring(value, axis, beside):
    size = lax.axis_size(axis)
    up = [(i, (i + 1) % size) for i in range(size)]
    down = [(i, (i - 1) % size) for i in range(size)]
    half = value.shape[0] // 2
    low, high = value[:half], value[half:]
    up_low = lax.ppermute(low, axis, up)
    down_high = lax.ppermute(high, axis, down)
    up_high = lax.ppermute(high, axis, up)
    down_low = lax.ppermute(low, axis, down)
    up_low, down_high, made = lax.optimization_barrier((up_low, down_high, beside()))
    far_up = lax.ppermute(up_low, axis, up)
    far_down = lax.ppermute(down_high, axis, down)
    return (value, up_low, up_high, down_low, down_high, far_up, far_down), made


def per_device(ancestor_inverse, fill_mask, block_order, l_rows, diag_inverse):
    snodes, tile = diag_inverse.shape[0], diag_inverse.shape[1]
    local_rows, local_cols = ancestor_inverse.shape
    blocks = block_order.shape[1]
    cols = NL * NY
    share = blocks // cols
    width = snodes * tile
    bf16 = jnp.bfloat16
    pos = jnp.stack([lax.axis_index(name) for name in ("x", "z", "l", "y")]).astype(jnp.int32)

    spread = pl.pallas_call(
        spread_kernel,
        out_shape=jax.ShapeDtypeStruct((NX * cols, snodes, SLICE, LANES), bf16),
        in_specs=[whole(SMEM), whole()],
        out_specs=whole(),
        compiler_params=params(),
        name="spread",
    )(pos, l_rows)
    got = lax.all_to_all(spread, ("x", "l", "y"), 0, 0, tiled=True)
    mine = pl.pallas_call(
        compact_kernel,
        out_shape=jax.ShapeDtypeStruct((blocks // NZ * snodes, SLICE, LANES), bf16),
        in_specs=[whole(SMEM), whole(pl.ANY), whole()],
        out_specs=whole(),
        compiler_params=params(),
        name="compact",
    )(pos, block_order, got)
    half_cols = local_cols // 2

    def gate(own_half, after):
        return pl.pallas_call(
            functools.partial(gate_kernel, own_half),
            out_shape=jax.ShapeDtypeStruct((local_rows, half_cols), bf16),
            in_specs=[whole(SMEM), whole(SMEM), whole(pl.ANY), whole(pl.ANY)],
            out_specs=whole(),
            scratch_shapes=[pltpu.SemaphoreType.DMA((share,))],
            compiler_params=params(),
            cost_estimate=pl.CostEstimate(
                flops=local_rows * half_cols, bytes_accessed=4 * local_rows * half_cols, transcendentals=0
            ),
            name="gate",
        )(pos, fill_mask, ancestor_inverse, after)

    everything = jnp.concatenate(ring(mine, "z"), axis=0)
    routed = pl.pallas_call(
        route_kernel,
        out_shape=jax.ShapeDtypeStruct((blocks, snodes, SLICE, LANES), bf16),
        in_specs=[whole(SMEM), whole(SMEM), whole()],
        out_specs=whole(),
        compiler_params=params(),
        name="route",
    )(pos, block_order, everything)
    quarters = lax.all_to_all(routed, ("l", "y"), 0, 0, tiled=True)
    own = pl.pallas_call(
        normal_kernel,
        out_shape=jax.ShapeDtypeStruct((share * NY * SLICE, width), bf16),
        in_specs=[whole(), whole()],
        out_specs=whole(),
        scratch_shapes=[VMEM((share * NY * SLICE, tile), bf16)],
        compiler_params=params(),
        name="normal",
    )(quarters.reshape(cols, share, snodes, SLICE, LANES), diag_inverse)
    (own, *near, far_up, far_down), gated_own = split_ring(own, "x", lambda: gate(True, own))
    gated_other = gate(False, own)
    near_value, begun = pl.pallas_call(
        near_kernel,
        out_shape=(
            jax.ShapeDtypeStruct((local_rows, width), jnp.float32),
            jax.ShapeDtypeStruct((half_cols, width), bf16),
        ),
        in_specs=[whole(SMEM)] + [whole()] * 6,
        out_specs=(whole(), whole()),
        scratch_shapes=[VMEM((half_cols, width), bf16)],
        compiler_params=params(),
        cost_estimate=pl.CostEstimate(
            flops=local_rows * local_cols * width, bytes_accessed=0, transcendentals=0
        ),
        name="near",
    )(pos, gated_other, own, *near)
    partial_value, _ = pl.pallas_call(
        far_kernel,
        out_shape=(
            jax.ShapeDtypeStruct((local_rows, width), bf16),
            jax.ShapeDtypeStruct((half_cols, width), bf16),
        ),
        in_specs=[whole(SMEM)] + [whole()] * 5,
        out_specs=(whole(), whole()),
        input_output_aliases={3: 1},
        compiler_params=params(),
        name="far",
    )(pos, gated_own, near_value, begun, far_up, far_down)
    share_rows = local_rows // cols
    shares = lax.all_to_all(partial_value, ("l", "y"), 0, 0, tiled=True)
    summed = shares.reshape(cols, share_rows, snodes, tile).astype(jnp.float32).sum(0)
    return summed.transpose(1, 2, 0).astype(bf16)


def solution(mesh):
    fine = Mesh(
        mesh.devices.reshape(NX, NZ, NL, NY, mesh.shape["snode"]), ("x", "z", "l", "y", "snode")
    )
    row, col = ("x", "z"), ("l", "y")
    return jax.shard_map(
        per_device,
        mesh=fine,
        in_specs=(
            P(("snode", *row), col),
            P("snode", None),
            P("snode", None),
            P("snode", (*row, *col), None),
            P("snode", None, None),
        ),
        out_specs=P("snode", None, (*row, *col)),
        check_vma=False,
    )
```

```python
import functools

import jax
import jax.numpy as jnp
from jax import lax
from jax.experimental import pallas as pl
from jax.experimental.pallas import tpu as pltpu
from jax.sharding import Mesh
from jax.sharding import PartitionSpec as P

NX, NZ, NL, NY = 4, 4, 2, 4
SLICE = 16
LANES = 128
VMEM = pltpu.VMEM
SMEM = pltpu.SMEM


def whole(space=VMEM):
    return pl.BlockSpec(memory_space=space)


def params():
    return pltpu.CompilerParams(vmem_limit_bytes=24 * 1024 * 1024)


def place_of(x):
    return ((x & 1) * 2 + x // 2) * NY


def spread_kernel(pos_ref, l_ref, out_ref):
    snodes, rows, _ = l_ref.shape
    count = rows // SLICE
    first = (pos_ref[2] * NY + pos_ref[3]) * count
    for i in range(count):
        k = (first + i) & (NX * NY - 1)
        for l in range(NL):
            x = ((k // NY) & 1) * 2 + k // (2 * NY)
            slot = (x * NL + l) * NY + (k & (NY - 1))
            for s in range(snodes):
                out_ref[slot, s] = l_ref[s, i * SLICE : (i + 1) * SLICE, l * LANES : (l + 1) * LANES]


def compact_kernel(pos_ref, _order, got_ref, out_ref):
    snodes = got_ref.shape[1]
    per_row = out_ref.shape[0] // (NX * snodes)
    count = per_row * NX * NY // (NL * NY)
    k = place_of(pos_ref[0]) + pos_ref[3]
    for t in range(per_row):
        col = (t * NX * NY + k) // count
        for x in range(NX):
            for s in range(snodes):
                out_ref[(x * per_row + t) * snodes + s] = got_ref[x * NL * NY + col, s]


def route_kernel(pos_ref, order_ref, all_ref, out_ref):
    snodes, blocks = order_ref.shape
    per_row = blocks // (NX * NZ)
    part = NX * per_row * snodes
    for z in range(NZ):
        d = (z - pos_ref[1]) & (NZ - 1)
        base = jnp.where(d == 0, 0, jnp.where(d == 3, 1, jnp.where(d == 1, 2, 3))) * part
        for x in range(NX):
            for t in range(per_row):
                q = (x * NZ + z) * per_row + t
                for s in range(snodes):
                    out_ref[order_ref[s, q], s] = all_ref[base + (x * per_row + t) * snodes + s]


def normal_kernel(got_ref, diag_ref, out_ref, picked):
    _, share, snodes = got_ref.shape[:3]
    tile = diag_ref.shape[1]
    for s in range(snodes):
        for a in range(share):
            for y in range(NY):
                at = (a * NY + y) * SLICE
                for l in range(NL):
                    picked[at : at + SLICE, l * LANES : (l + 1) * LANES] = got_ref[l * NY + y, a, s]
        out_ref[:, s * tile : (s + 1) * tile] = jnp.dot(
            picked[...], diag_ref[s], preferred_element_type=jnp.float32
        ).astype(out_ref.dtype)


def fill(stacked, pairs):
    quarter = NY * SLICE
    share = stacked.shape[0] // (2 * quarter)
    for x, refs in pairs:
        each = share // len(refs)
        for a in range(share):
            at = pl.multiple_of(a * 2 * quarter + (x // 2) * quarter, quarter)
            n = a % each
            stacked[pl.ds(at, quarter), :] = refs[a // each][n * quarter : (n + 1) * quarter, :]


def gate_kernel(own_half, pos_ref, mask_ref, a_ref, _after, out_ref, arrived):
    rows, half = out_ref.shape
    share = half // LANES
    tile = 2 * LANES
    x = pos_ref[0]
    side = (x & 1) if own_half else 1 - (x & 1)
    copies = []
    for a in range(share):
        columns = pl.ds(pl.multiple_of(a * tile + side * LANES, LANES), LANES)
        copies.append(
            pltpu.make_async_copy(a_ref.at[:, columns], out_ref.at[:, a * LANES : (a + 1) * LANES], arrived.at[a])
        )
        copies[a].start()
    row = (x * NZ + pos_ref[1]) * (rows // tile)
    col = (pos_ref[2] * NY + pos_ref[3]) * share
    for a in range(share):
        copies[a].wait()
        at = slice(a * LANES, (a + 1) * LANES)
        for i in range(rows // tile):
            keep = jnp.full((1, LANES), mask_ref[row + i, col + a], jnp.int32).astype(jnp.float32)
            down = slice(i * tile, (i + 1) * tile)
            out_ref[down, at] = out_ref[down, at] * keep.astype(jnp.bfloat16)


def near_kernel(pos_ref, a_ref, ul_ref, uh_ref, dl_ref, dh_ref, out_ref, stacked):
    x = pos_ref[0]
    fill(stacked, (((x - 1) & (NX - 1), (ul_ref, uh_ref)), ((x + 1) & (NX - 1), (dl_ref, dh_ref))))
    tile = 2 * LANES
    for n in range(out_ref.shape[1] // tile):
        at = slice(n * tile, (n + 1) * tile)
        out_ref[:, at] = jnp.dot(a_ref[...], stacked[:, at], preferred_element_type=jnp.float32)


def far_kernel(pos_ref, a_ref, near_ref, own_ref, fu_ref, fd_ref, out_ref, stacked):
    x = pos_ref[0]
    fill(stacked, ((x, (own_ref,)), ((x + 2) & (NX - 1), (fu_ref, fd_ref))))
    tile = 2 * LANES
    for n in range(out_ref.shape[1] // tile):
        at = slice(n * tile, (n + 1) * tile)
        out_ref[:, at] = (
            -(near_ref[:, at] + jnp.dot(a_ref[...], stacked[:, at], preferred_element_type=jnp.float32))
        ).astype(out_ref.dtype)


def ring(value, axis):
    size = lax.axis_size(axis)
    up = [(i, (i + 1) % size) for i in range(size)]
    down = [(i, (i - 1) % size) for i in range(size)]
    half = value.shape[0] // 2
    from_up = lax.ppermute(value, axis, up)
    from_down = lax.ppermute(value, axis, down)
    far_up = lax.ppermute(from_up[:half], axis, up)
    far_down = lax.ppermute(from_down[half:], axis, down)
    return value, from_up, from_down, far_up, far_down


def split_ring(value, axis, beside):
    size = lax.axis_size(axis)
    up = [(i, (i + 1) % size) for i in range(size)]
    down = [(i, (i - 1) % size) for i in range(size)]
    half = value.shape[0] // 2
    low, high = value[:half], value[half:]
    up_low = lax.ppermute(low, axis, up)
    down_high = lax.ppermute(high, axis, down)
    up_high = lax.ppermute(high, axis, up)
    down_low = lax.ppermute(low, axis, down)
    up_low, down_high, made = lax.optimization_barrier((up_low, down_high, beside()))
    far_up = lax.ppermute(up_low, axis, up)
    far_down = lax.ppermute(down_high, axis, down)
    return (value, up_low, up_high, down_low, down_high, far_up, far_down), made


def per_device(ancestor_inverse, fill_mask, block_order, l_rows, diag_inverse):
    snodes, tile = diag_inverse.shape[0], diag_inverse.shape[1]
    local_rows, local_cols = ancestor_inverse.shape
    blocks = block_order.shape[1]
    cols = NL * NY
    share = blocks // cols
    width = snodes * tile
    bf16 = jnp.bfloat16
    pos = jnp.stack([lax.axis_index(name) for name in ("x", "z", "l", "y")]).astype(jnp.int32)

    spread = pl.pallas_call(
        spread_kernel,
        out_shape=jax.ShapeDtypeStruct((NX * cols, snodes, SLICE, LANES), bf16),
        in_specs=[whole(SMEM), whole()],
        out_specs=whole(),
        compiler_params=params(),
        name="spread",
    )(pos, l_rows)
    got = lax.all_to_all(spread, ("x", "l", "y"), 0, 0, tiled=True)
    mine = pl.pallas_call(
        compact_kernel,
        out_shape=jax.ShapeDtypeStruct((blocks // NZ * snodes, SLICE, LANES), bf16),
        in_specs=[whole(SMEM), whole(pl.ANY), whole()],
        out_specs=whole(),
        compiler_params=params(),
        name="compact",
    )(pos, block_order, got)
    half_cols = local_cols // 2

    def gate(own_half, after):
        return pl.pallas_call(
            functools.partial(gate_kernel, own_half),
            out_shape=jax.ShapeDtypeStruct((local_rows, half_cols), bf16),
            in_specs=[whole(SMEM), whole(SMEM), whole(pl.ANY), whole(pl.ANY)],
            out_specs=whole(),
            scratch_shapes=[pltpu.SemaphoreType.DMA((share,))],
            compiler_params=params(),
            cost_estimate=pl.CostEstimate(
                flops=local_rows * half_cols, bytes_accessed=4 * local_rows * half_cols, transcendentals=0
            ),
            name="gate",
        )(pos, fill_mask, ancestor_inverse, after)

    everything = jnp.concatenate(ring(mine, "z"), axis=0)
    routed = pl.pallas_call(
        route_kernel,
        out_shape=jax.ShapeDtypeStruct((blocks, snodes, SLICE, LANES), bf16),
        in_specs=[whole(SMEM), whole(SMEM), whole()],
        out_specs=whole(),
        compiler_params=params(),
        name="route",
    )(pos, block_order, everything)
    quarters = lax.all_to_all(routed, ("l", "y"), 0, 0, tiled=True)
    own = pl.pallas_call(
        normal_kernel,
        out_shape=jax.ShapeDtypeStruct((share * NY * SLICE, width), bf16),
        in_specs=[whole(), whole()],
        out_specs=whole(),
        scratch_shapes=[VMEM((share * NY * SLICE, tile), bf16)],
        compiler_params=params(),
        name="normal",
    )(quarters.reshape(cols, share, snodes, SLICE, LANES), diag_inverse)
    (own, *near, far_up, far_down), gated_own = split_ring(own, "x", lambda: gate(True, own))
    gated_other = gate(False, own)
    near_value = pl.pallas_call(
        near_kernel,
        out_shape=jax.ShapeDtypeStruct((local_rows, width), jnp.float32),
        in_specs=[whole(SMEM)] + [whole()] * 5,
        out_specs=whole(),
        scratch_shapes=[VMEM((half_cols, width), bf16)],
        compiler_params=params(),
        cost_estimate=pl.CostEstimate(
            flops=local_rows * local_cols * width, bytes_accessed=0, transcendentals=0
        ),
        name="near",
    )(pos, gated_other, *near)
    partial_value = pl.pallas_call(
        far_kernel,
        out_shape=jax.ShapeDtypeStruct((local_rows, width), bf16),
        in_specs=[whole(SMEM)] + [whole()] * 5,
        out_specs=whole(),
        scratch_shapes=[VMEM((half_cols, width), bf16)],
        compiler_params=params(),
        name="far",
    )(pos, gated_own, near_value, own, far_up, far_down)
    share_rows = local_rows // cols
    shares = lax.all_to_all(partial_value, ("l", "y"), 0, 0, tiled=True)
    summed = shares.reshape(cols, share_rows, snodes, tile).astype(jnp.float32).sum(0)
    return summed.transpose(1, 2, 0).astype(bf16)


def solution(mesh):
    fine = Mesh(
        mesh.devices.reshape(NX, NZ, NL, NY, mesh.shape["snode"]), ("x", "z", "l", "y", "snode")
    )
    row, col = ("x", "z"), ("l", "y")
    return jax.shard_map(
        per_device,
        mesh=fine,
        in_specs=(
            P(("snode", *row), col),
            P("snode", None),
            P("snode", None),
            P("snode", (*row, *col), None),
            P("snode", None, None),
        ),
        out_specs=P("snode", None, (*row, *col)),
        check_vma=False,
    )
```
